256 devices in a mesh: row: 16 (over y_lo, x, core), col: 16 (over z, y_hi).
Axes of the slice: x: 4, y: 4 (y_hi: 2, y_lo: 2; y = y_hi * 2 + y_lo), z: 8, core: 2. Of those that a mesh axis runs over, the one named last changes fastest.
Arguments:
- tokens: int32 [1024], replicated, may hold values from 0 to 16383
- table: bfloat16 [16384, 12288], P('row', 'col'), may hold values from -6 to 6
- gate_weight: bfloat16 [12288, 14336], P('col', 'row'), may hold values from -0.0546875 to 0.0546875
- up_weight: bfloat16 [12288, 14336], P('col', 'row'), may hold values from -0.0546875 to 0.0546875
- down_weight: bfloat16 [14336, 12288], P('row', 'col'), may hold values from -0.046875 to 0.046875
- gate_left: bfloat16 [12288, 64], P(('col', 'row')), may hold values from -0.0546875 to 0.0546875
- gate_right: bfloat16 [64, 14336], P(None, ('row', 'col')), may hold values from -0.3125 to 0.3125
- up_left: bfloat16 [12288, 64], P(('col', 'row')), may hold values from -0.0546875 to 0.0546875
- up_right: bfloat16 [64, 14336], P(None, ('row', 'col')), may hold values from -0.3125 to 0.3125
- down_left: bfloat16 [14336, 64], P(('row', 'col')), may hold values from -0.046875 to 0.046875
- down_right: bfloat16 [64, 12288], P(None, ('col', 'row')), may hold values from -0.3125 to 0.3125
Outputs:
- canary: float32 [1024, 12288], P('row', 'col')
- merged_gate: bfloat16 [12288, 14336], P('col', 'row')
- merged_up: bfloat16 [12288, 14336], P('col', 'row')
- merged_down: bfloat16 [14336, 12288], P('row', 'col')
The draws below stay inside these ranges and needn't reach their ends.
All inputs are finite; a program needn't handle non-finite values.
Results may differ from the reference program's by a relative error of at most 0.0065.
Values may be sent and summed in bfloat16 or wider, within the bound.
No kernel may reach another device: no remote copies, remote signals or barrier semaphores. Data moves between devices by JAX's collectives and lax.ppermute only.
A program may use at most 64 MiB of HBM per device.

```python
import jax
import jax.numpy as jnp

D = 12288
FF = 14336
VOCAB = 16384
RANK = 64
ROWS = 1024


def plant(entries, key, low, largest):
    place = [jax.random.randint(jax.random.fold_in(key, axis), (), 0, length) for axis, length in enumerate(entries.shape)]
    main_axis = entries.shape.index(max(entries.shape))
    beside = place[:main_axis] + [(place[main_axis] + 1) % entries.shape[main_axis]] + place[main_axis + 1:]
    return entries.at[tuple(place)].set(low).at[tuple(beside)].set(largest)


def block_levels(rng, shape, split, low, top_value):
    level = 1.0
    for axis_at, parts in split:
        heights = jax.random.uniform(jax.random.fold_in(jax.random.fold_in(rng, 6), axis_at), (parts,), jnp.float32, low / len(split), top_value / len(split))
        level = level * jnp.repeat(jnp.exp(heights), shape[axis_at] // parts).reshape((-1,) + (1,) * (len(shape) - 1 - axis_at))
    return level


def bell_draw(key, shape, deviation, bound, shards=(), kind=jnp.bfloat16):
    loudness = block_levels(key, shape, shards, -0.22, 0.18) if shards else 1.0
    array = jax.random.normal(key, shape, jnp.float32) * deviation * loudness
    return jnp.minimum(jnp.maximum(array, -bound), bound).astype(kind)


def setup_inputs(seed: int = 0) -> dict:
    splits = jax.random.split(jax.random.key(seed), 12)
    return {
        "tokens": plant(jax.random.randint(splits[0], (ROWS,), 0, VOCAB), jax.random.fold_in(splits[0], 1), 0, VOCAB - 1).astype(jnp.int32),
        "table": bell_draw(splits[1], (VOCAB, D), 1.0, 6.0, ((0, 16), (1, 16))),
        "gate_weight": bell_draw(splits[2], (D, FF), D ** -0.5, 0.0546875, ((0, 16), (1, 16))),
        "up_weight": bell_draw(splits[3], (D, FF), D ** -0.5, 0.0546875, ((0, 16), (1, 16))),
        "down_weight": bell_draw(splits[4], (FF, D), FF ** -0.5, 0.046875, ((0, 16), (1, 16))),
        "gate_left": bell_draw(splits[5], (D, RANK), D ** -0.5, 0.0546875, ((0, 256),)),
        "gate_right": bell_draw(splits[6], (RANK, FF), 0.02, 0.3125, ((1, 256),)),
        "up_left": bell_draw(splits[7], (D, RANK), D ** -0.5, 0.0546875, ((0, 256),)),
        "up_right": bell_draw(splits[8], (RANK, FF), 0.02, 0.3125, ((1, 256),)),
        "down_left": bell_draw(splits[9], (FF, RANK), FF ** -0.5, 0.046875, ((0, 256),)),
        "down_right": bell_draw(splits[10], (RANK, D), 0.02, 0.3125, ((1, 256),)),
    }


def merge_tile(weight, left, right):
    delta = jnp.dot(left, right, preferred_element_type=jnp.float32)
    return (weight.astype(jnp.float32) + 2.0 * delta).astype(jnp.bfloat16)


def reference(tokens, table, gate_weight, up_weight, down_weight, gate_left, gate_right, up_left, up_right, down_left, down_right):
    merged_gate = merge_tile(gate_weight, gate_left, gate_right)
    merged_up = merge_tile(up_weight, up_left, up_right)
    merged_down = merge_tile(down_weight, down_left, down_right)
    embedded = jnp.take(table, tokens, axis=0)
    gate = jnp.dot(embedded, merged_gate, preferred_element_type=jnp.float32)
    up = jnp.dot(embedded, merged_up, preferred_element_type=jnp.float32)
    hidden = (jax.nn.silu(gate) * up).astype(jnp.bfloat16)
    canary = jnp.dot(hidden, merged_down, preferred_element_type=jnp.float32)
    return canary, merged_gate, merged_up, merged_down
```

```python
import jax
import jax.numpy as jnp
from jax import lax
from jax.sharding import PartitionSpec as P

BF16 = jnp.bfloat16
F32 = jnp.float32

NX, NZ, NB = 4, 8, 16
CHUNKS = 1


def row_perm(dy=0, dx=0, dc=0):
    return [
        (
            (y * NX + x) * 2 + c,
            ((y ^ dy) * NX + (x + dx) % NX) * 2 + (c ^ dc),
        )
        for y in range(2)
        for x in range(NX)
        for c in range(2)
    ]


def col_perm(dz=0, dy=0):
    return [
        (z * 2 + y, ((z + dz) % NZ) * 2 + (y ^ dy)) for z in range(NZ) for y in range(2)
    ]


def xor_perm(mask):
    return [(i, i ^ mask) for i in range(NB)]


def send_row(value, **kw):
    return lax.ppermute(value, "row", row_perm(**kw))


def send_col(value, **kw):
    return lax.ppermute(value, "col", col_perm(**kw))


def gather_small(piece, axis):
    index = lax.axis_index(axis)
    held = piece[None]
    for bit in range(4):
        other = lax.ppermute(held, axis, xor_perm(1 << bit))
        low = (index >> bit) & 1 == 0
        held = jnp.concatenate(
            [jnp.where(low, held, other), jnp.where(low, other, held)], axis=0
        )
    return held


def merge_tile(weight, left, right):
    delta = jnp.dot(left, right, preferred_element_type=F32)
    return (weight.astype(F32) + 2.0 * delta).astype(BF16)


def lookup(ids, table):
    vocab = table.shape[0]
    local = ids - lax.axis_index("row") * vocab
    hot = (local[:, None] == lax.broadcasted_iota(jnp.int32, (1, vocab), 1)).astype(BF16)
    return jnp.dot(hot, table, preferred_element_type=F32).astype(BF16)


def embed(ids, table):
    n = ids.shape[0]
    m = n // NB
    term = lookup(ids, table)
    half = term[: n // 2] + send_row(term[n // 2 :], dc=1)
    q = n // 8
    parts = [half[:q]] + [
        send_row(half[d * q : (d + 1) * q], dx=d) for d in range(1, NX)
    ]
    mine = parts[0] + parts[1] + parts[2] + parts[3]
    other = send_row(mine, dy=1)
    mine = mine + jnp.concatenate([other[m:], other[:m]], axis=0)
    half = jnp.concatenate(
        [mine] + [send_row(mine, dx=-d) for d in range(1, NX)], axis=0
    )
    return jnp.concatenate([half, send_row(half, dc=1)], axis=0)


def block(value, index, size):
    return lax.dynamic_slice_in_dim(value, (index % NZ) * size, size, axis=0)


def ring_scatter(part, z, sign):
    b = part.shape[0] // NZ
    far = block(part, z + 4 * sign, b).astype(BF16)
    up = send_col(far, dz=sign)
    down = None
    for d in (3, 2, 1):
        up_next = (block(part, z + d * sign, b) + up).astype(BF16)
        mine = block(part, z - d * sign, b)
        down_next = (mine if down is None else mine + down).astype(BF16)
        up = send_col(up_next, dz=sign)
        down = send_col(down_next, dz=-sign)
    return block(part, z, b) + up + down


def ring_gather(piece, z, sign):
    b = piece.shape[0]
    out = jnp.zeros((NZ * b,) + piece.shape[1:], piece.dtype)

    def put(out, value, index):
        return lax.dynamic_update_slice_in_dim(out, value, (index % NZ) * b, axis=0)

    out = put(out, piece, z)
    up = down = piece
    for d in (1, 2, 3):
        up = send_col(up, dz=sign)
        down = send_col(down, dz=-sign)
        out = put(out, up, z - d * sign)
        out = put(out, down, z + d * sign)
    up = send_col(up, dz=sign)
    return put(out, up, z - 4 * sign)


def activate(total):
    w = total.shape[1] // 2
    gate, up = total[:, :w], total[:, w:]
    return (jax.nn.silu(gate) * up).astype(BF16)


def swiglu_z_first(part, z, y, sign):
    m = part.shape[0] // NB
    both = ring_scatter(part, z, sign)
    theirs = lax.dynamic_slice_in_dim(both, (1 - y) * m, m, axis=0).astype(BF16)
    mine = lax.dynamic_slice_in_dim(both, y * m, m, axis=0)
    hidden = activate(mine + send_col(theirs, dy=1))
    other = send_col(hidden, dy=1)
    low = y == 0
    pair = jnp.concatenate(
        [jnp.where(low, hidden, other), jnp.where(low, other, hidden)], axis=0
    )
    return ring_gather(pair, z, sign)


def swiglu_y_first(part, z, y, sign):
    h = part.shape[0] // 2
    theirs = lax.dynamic_slice_in_dim(part, (1 - y) * h, h, axis=0).astype(BF16)
    mine = lax.dynamic_slice_in_dim(part, y * h, h, axis=0)
    mine = mine + send_col(theirs, dy=1)
    hidden = ring_gather(activate(ring_scatter(mine, z, sign)), z, sign)
    other = send_col(hidden, dy=1)
    low = y == 0
    return jnp.concatenate(
        [jnp.where(low, hidden, other), jnp.where(low, other, hidden)], axis=0
    )


def scatter_rows(part):
    n = part.shape[0]
    m, q = n // NB, n // 8
    half = part[: n // 2] + send_row(part[n // 2 :].astype(BF16), dc=1)
    parts = [half[:q]] + [
        send_row(half[d * q : (d + 1) * q].astype(BF16), dx=d) for d in range(1, NX)
    ]
    mine = parts[0] + parts[1] + parts[2] + parts[3]
    return mine[:m] + send_row(mine[m:].astype(BF16), dy=1)


def relative_tokens(tokens):
    row = lax.axis_index("row")
    core, x, y = row % 2, (row // 2) % NX, row // (2 * NX)
    m = tokens.shape[0] // (NB * CHUNKS)
    ids = tokens.reshape(2, NX, 2, CHUNKS, m)
    order = (jnp.arange(2) + y) % 2
    ids = jnp.take(ids, order, axis=0)
    ids = jnp.take(ids, (jnp.arange(NX) + x) % NX, axis=1)
    ids = jnp.take(ids, (jnp.arange(2) + core) % 2, axis=2)
    return ids.transpose(3, 2, 1, 0, 4).reshape(CHUNKS, NB * m)


def per_device(
    tokens,
    table,
    gate_weight,
    up_weight,
    down_weight,
    gate_left,
    gate_right,
    up_left,
    up_right,
    down_left,
    down_right,
):
    col = lax.axis_index("col")
    z, y = col // 2, col % 2
    ids = relative_tokens(tokens)

    a, b = gate_left.shape[0], gate_right.shape[1]
    width = gather_small(
        jnp.concatenate([gate_left, up_left, down_right.T], axis=0), "row"
    )
    units = gather_small(
        jnp.concatenate([gate_right.T, up_right.T, down_left], axis=0), "col"
    )
    gate_l, up_l, down_r = (
        width[:, i * a : (i + 1) * a].reshape(-1, width.shape[-1]) for i in range(3)
    )
    gate_r, up_r, down_l = (
        units[:, i * b : (i + 1) * b].reshape(-1, units.shape[-1]) for i in range(3)
    )
    merged_gate = merge_tile(gate_weight, gate_l, gate_r.T)
    merged_up = merge_tile(up_weight, up_l, up_r.T)
    merged_down = merge_tile(down_weight, down_l, down_r.T)
    both = jnp.concatenate([merged_gate, merged_up], axis=1)

    outs = []
    for k in range(CHUNKS):
        embedded = embed(ids[k], table)
        part = jnp.dot(embedded, both, preferred_element_type=F32)
        if k % 2 == 0:
            hidden = swiglu_z_first(part, z, y, 1)
        else:
            hidden = swiglu_y_first(part, z, y, -1)
        outs.append(
            scatter_rows(jnp.dot(hidden, merged_down, preferred_element_type=F32))
        )
    result = jnp.concatenate(outs, axis=0)
    return (result, merged_gate, merged_up, merged_down)


def solution(mesh):
    in_specs = (
        P(),
        P("row", "col"),
        P("col", "row"),
        P("col", "row"),
        P("row", "col"),
        P(("col", "row"), None),
        P(None, ("row", "col")),
        P(("col", "row"), None),
        P(None, ("row", "col")),
        P(("row", "col"), None),
        P(None, ("col", "row")),
    )
    out_specs = (P("row", "col"), P("col", "row"), P("col", "row"), P("row", "col"))
    return jax.shard_map(
        per_device, mesh=mesh, in_specs=in_specs, out_specs=out_specs, check_vma=False
    )
```

```python
import jax
import jax.numpy as jnp
from jax import lax
from jax.sharding import Mesh, PartitionSpec as P

BF16 = jnp.bfloat16
F32 = jnp.float32

NZ = 8
ROW = ("yl", "x", "core")
COL = ("z", "yh")
RING = True
STREAMS = 2


def shift(n, d):
    return [(i, (i + d) % n) for i in range(n)]


def flip(n, mask):
    return [(i, i ^ mask) for i in range(n)]


def swap(value, axis):
    return lax.ppermute(value, axis, flip(2, 1))


def gather_small(held, axes):
    for axis, size in axes:
        index = lax.axis_index(axis)
        for bit in range(size.bit_length() - 1):
            other = lax.ppermute(held, axis, flip(size, 1 << bit))
            low = (index >> bit) & 1 == 0
            held = jnp.concatenate(
                [jnp.where(low, held, other), jnp.where(low, other, held)], axis=0
            )
    return held


def merge_tile(weight, left, right):
    delta = jnp.dot(left, right, preferred_element_type=F32)
    return (weight.astype(F32) + 2.0 * delta).astype(BF16)


def lookup(ids, table, base):
    local = ids - base
    hot = (local[:, None] == lax.broadcasted_iota(jnp.int32, (1, table.shape[0]), 1)).astype(BF16)
    return jnp.dot(hot, table, preferred_element_type=F32).astype(BF16)


def exchange(value):
    return lax.all_to_all(value, ("yl", "x"), 0, 0)


def pack(piece, width):
    groups = [piece[16 * k : 16 * (k + 1)] for k in range(piece.shape[0] // 16)]
    flat = jnp.concatenate(groups, axis=1)
    return jnp.pad(flat, ((0, 0), (0, width - flat.shape[1])))


def unpack(packed, count, rank):
    per = 3
    return [
        jnp.concatenate(
            [
                packed[:, :, rank * (per * i + k) : rank * (per * i + k + 1)]
                for k in range(per)
            ],
            axis=1,
        )
        for i in range(count)
    ]


def embed(tokens, table, extra):
    core = lax.axis_index("core")
    base = lax.axis_index(ROW) * table.shape[0]
    m = tokens.shape[0] // 16
    ids = tokens.reshape(8, 2, m)

    def of(c):
        return lax.dynamic_index_in_dim(ids, c, axis=1, keepdims=False).reshape(-1)

    theirs = lookup(of(1 - core), table, base)
    got = swap(theirs, "core")
    half = lookup(of(core), table, base) + got
    pieces = exchange(half.reshape(8, m, -1))
    mine = pieces[0]
    for j in range(1, 8):
        mine = mine + pieces[j]
    mine = jnp.concatenate([mine, extra], axis=0)
    every = exchange(jnp.broadcast_to(mine[None], (8,) + mine.shape))
    return every[:, :m].reshape(8 * m, -1), every[:, m:]


def block(value, index, size):
    return lax.dynamic_slice_in_dim(value, (index % NZ) * size, size, axis=0)


def ring_scatter(part, z, sign):
    b = part.shape[0] // NZ
    up_perm, down_perm = shift(NZ, sign), shift(NZ, -sign)
    up = lax.ppermute(block(part, z + 4 * sign, b).astype(BF16), "z", up_perm)
    down = None
    for d in (3, 2, 1):
        up_next = (block(part, z + d * sign, b) + up).astype(BF16)
        mine = block(part, z - d * sign, b)
        down_next = (mine if down is None else mine + down).astype(BF16)
        up = lax.ppermute(up_next, "z", up_perm)
        down = lax.ppermute(down_next, "z", down_perm)
    return block(part, z, b) + up + down


def ring_gather(piece, z, sign):
    b = piece.shape[0]
    up_perm, down_perm = shift(NZ, sign), shift(NZ, -sign)
    out = jnp.zeros((NZ * b,) + piece.shape[1:], piece.dtype)

    def put(out, value, index):
        return lax.dynamic_update_slice_in_dim(out, value, (index % NZ) * b, axis=0)

    out = put(out, piece, z)
    up = down = piece
    for d in (1, 2, 3):
        up = lax.ppermute(up, "z", up_perm)
        down = lax.ppermute(down, "z", down_perm)
        out = put(out, up, z - d * sign)
        out = put(out, down, z + d * sign)
    h = b // 2
    up = lax.ppermute(up[:h], "z", up_perm)
    down = lax.ppermute(down[h:], "z", down_perm)
    return put(out, jnp.concatenate([up, down], axis=0), z - 4 * sign)


def activate(gate, up):
    return (jax.nn.silu(gate) * up).astype(BF16)


def times_t(a, b):
    return lax.dot_general(
        a,
        b.astype(F32),
        (((1,), (1,)), ((), ())),
        precision=lax.Precision.HIGHEST,
        preferred_element_type=F32,
    )


def scatter_rows(part):
    n = part.shape[0]
    pieces = exchange(part.astype(BF16).reshape(8, n // 8, -1))
    return jnp.sum(pieces.astype(F32), axis=0)


def per_device(
    tokens,
    table,
    gate_weight,
    up_weight,
    down_weight,
    gate_left,
    gate_right,
    up_left,
    up_right,
    down_left,
    down_right,
):
    z = lax.axis_index("z")
    first = lax.axis_index("core") == 0
    b, rank = gate_right.shape[1], gate_right.shape[0]
    ff = gate_weight.shape[1]

    width = pack(
        jnp.concatenate([gate_left, up_left, down_right.T], axis=0), table.shape[1]
    )
    gate_other, up_other = swap(gate_weight, "core"), swap(up_weight, "core")
    weights = jnp.concatenate([gate_weight, up_weight, gate_other, up_other], axis=1)
    embedded, width = embed(tokens, table, width)
    width_other = swap(width, "core")
    width = jnp.stack(
        [jnp.where(first, width, width_other), jnp.where(first, width_other, width)],
        axis=1,
    ).reshape((16,) + width.shape[1:])
    gate_l, up_l, down_r = (
        p.reshape(-1, rank) for p in unpack(width, 3, rank)
    )

    n = embedded.shape[0]
    left = jnp.concatenate([gate_l, up_l], axis=1)
    low = jnp.dot(embedded, left, preferred_element_type=F32)
    part = jnp.dot(embedded, weights, preferred_element_type=F32)

    units = gather_small(
        jnp.concatenate([gate_right.T, up_right.T, down_left], axis=0)[None],
        (("yh", 2), ("z", 8)),
    )
    units_other = swap(units[:, : 2 * b], "core")
    gate_r, up_r, down_l = (
        units[:, i * b : (i + 1) * b].reshape(-1, rank) for i in range(3)
    )
    gate_ro, up_ro = (
        units_other[:, i * b : (i + 1) * b].reshape(-1, rank) for i in range(2)
    )
    merged_gate = merge_tile(gate_weight, gate_l, gate_r.T)
    merged_up = merge_tile(up_weight, up_l, up_r.T)
    merged_down = merge_tile(down_weight, down_l, down_r.T)
    down = jnp.concatenate([merged_down, swap(merged_down, "core")], axis=0)

    streams = []
    for k in range(STREAMS):
        rows = slice(k * n // STREAMS, (k + 1) * n // STREAMS)
        sums = jnp.concatenate([part[rows], low[rows]], axis=1)
        sign = 1 - 2 * (k % 2)
        if RING:
            mine = ring_scatter(sums, z, sign)
        else:
            mine = lax.psum_scatter(
                sums.astype(BF16), "z", scatter_dimension=0, tiled=True
            ).astype(F32)
        total = mine + swap(mine.astype(BF16), "yh")
        gate, up, gate_o, up_o = (total[:, i * ff : (i + 1) * ff] for i in range(4))
        gate_t, up_t = 2.0 * total[:, -2 * rank : -rank], 2.0 * total[:, -rank:]
        hidden = jnp.concatenate(
            [
                activate(gate + times_t(gate_t, gate_r), up + times_t(up_t, up_r)),
                activate(gate_o + times_t(gate_t, gate_ro), up_o + times_t(up_t, up_ro)),
            ],
            axis=1,
        )
        streams.append(ring_gather(hidden, z, sign))
    hidden = jnp.concatenate(streams, axis=0)
    result = scatter_rows(jnp.dot(hidden, down, preferred_element_type=F32))
    return (result, merged_gate, merged_up, merged_down)


def solution(mesh):
    fine = Mesh(mesh.devices.reshape(2, 4, 2, NZ, 2), ROW + COL)
    in_specs = (
        P(),
        P(ROW, COL),
        P(COL, ROW),
        P(COL, ROW),
        P(ROW, COL),
        P(COL + ROW, None),
        P(None, ROW + COL),
        P(COL + ROW, None),
        P(None, ROW + COL),
        P(ROW + COL, None),
        P(None, COL + ROW),
    )
    out_specs = (P(ROW, COL), P(COL, ROW), P(COL, ROW), P(ROW, COL))
    return jax.shard_map(
        per_device, mesh=fine, in_specs=in_specs, out_specs=out_specs, check_vma=False
    )
```

```python
import jax
import jax.numpy as jnp
from jax import lax
from jax.sharding import Mesh, PartitionSpec as P

BF16 = jnp.bfloat16
F32 = jnp.float32

NX, NZ = 4, 8
ROW = ("yl", "x", "core")
COL = ("z", "yh")


def shift(n, d):
    return [(i, (i + d) % n) for i in range(n)]


def flip(n, mask):
    return [(i, i ^ mask) for i in range(n)]


def swap(value, axis):
    return lax.ppermute(value, axis, flip(2, 1))


def after(value, *others):
    return lax.optimization_barrier((value, *others))[0]


def put(out, value, index):
    return lax.dynamic_update_index_in_dim(out, value, index % out.shape[0], 0)


def merge_tile(weight, left, right):
    delta = jnp.dot(left, right, preferred_element_type=F32)
    return (weight.astype(F32) + 2.0 * delta).astype(BF16)


def lookup(ids, table, base):
    local = ids - base
    hot = (local[:, None] == lax.broadcasted_iota(jnp.int32, (1, table.shape[0]), 1)).astype(BF16)
    return jnp.dot(hot, table, preferred_element_type=F32).astype(BF16)


def exchange(value):
    return lax.all_to_all(value, ("yl", "x"), 0, 0)


def pack(piece, width):
    groups = [piece[16 * k : 16 * (k + 1)] for k in range(piece.shape[0] // 16)]
    flat = jnp.concatenate(groups, axis=1)
    return jnp.pad(flat, ((0, 0), (0, width - flat.shape[1])))


def unpack(packed, count, rank):
    per = 3
    return [
        jnp.concatenate(
            [
                packed[:, :, rank * (per * i + k) : rank * (per * i + k + 1)]
                for k in range(per)
            ],
            axis=1,
        ).reshape(-1, rank)
        for i in range(count)
    ]


def gather_units(pieces, late):
    low = lax.axis_index("yh") == 0
    other = swap(pieces, "yh")
    pair = [jnp.where(low, pieces, other), jnp.where(low, other, pieces)]
    held = jnp.concatenate(
        [jnp.concatenate([p[0], p[1]], axis=1) for p in pair]
        + [jnp.concatenate([pair[0][2], pair[1][2]], axis=1)],
        axis=0,
    )
    shape = held.shape
    for mask in (4, 2, 1):
        if mask == 2:
            held = after(held, late)
        other = lax.ppermute(held, "z", flip(NZ, mask))
        low = lax.axis_index("z") & mask == 0
        held = jnp.stack([jnp.where(low, held, other), jnp.where(low, other, held)])
    return held.transpose(2, 1, 0, 3, 4).reshape((NZ,) + shape)


def embed(tokens, table, table_other, extra):
    core = lax.axis_index("core")
    vocab, wide = table.shape
    base = lax.axis_index(ROW) * vocab
    other_base = base + (1 - 2 * core) * vocab
    m = tokens.shape[0] // 16

    ids = tokens.reshape(8, 2, m)
    ids = lax.dynamic_index_in_dim(ids, core, axis=1, keepdims=False).reshape(-1)
    half = lookup(ids, table, base) + lookup(ids, table_other, other_base)
    pieces = exchange(half.reshape(8, m, wide))
    mine = pieces[0]
    for j in range(1, 8):
        mine = mine + pieces[j]
    mine = jnp.concatenate([mine, extra], axis=0)
    copies = lax.optimization_barrier(jnp.broadcast_to(mine[None], (8,) + mine.shape))
    every = exchange(copies)
    extras = every[:, m:]
    extras_other = swap(extras, "core")
    first = core == 0
    extras = jnp.stack(
        [
            jnp.where(first, extras, extras_other),
            jnp.where(first, extras_other, extras),
        ],
        axis=1,
    )
    rows = lax.optimization_barrier(every[:, :m].reshape(8 * m, wide))
    return rows, extras.reshape((16,) + extra.shape), half, copies


def ring_scatter(columns, z, sign):
    columns = [c.reshape(NZ, c.shape[0] // NZ, -1) for c in columns]
    up_perm, down_perm = shift(NZ, sign), shift(NZ, -sign)

    def add(index, held):
        index = (index + NZ) % NZ
        blocks = [
            lax.dynamic_index_in_dim(c, index, 0, keepdims=False) for c in columns
        ]
        whole = jnp.concatenate(blocks, axis=1)
        return whole if held is None else whole + held

    up = lax.ppermute(add(z + 4, None).astype(BF16), "z", up_perm)
    down = None
    for d in (3, 2, 1):
        up_next = add(z + d * sign, up).astype(BF16)
        down_next = add(z - d * sign, down).astype(BF16)
        up = lax.ppermute(up_next, "z", up_perm)
        down = lax.ppermute(down_next, "z", down_perm)
    return add(z, up) + down


def ring_gather(piece, z, sign):
    b = piece.shape[0]
    up_perm, down_perm = shift(NZ, sign), shift(NZ, -sign)
    out = put(jnp.zeros((NZ,) + piece.shape, piece.dtype), piece, z)
    up = down = piece
    for d in (1, 2, 3):
        up = lax.ppermute(up, "z", up_perm)
        down = lax.ppermute(down, "z", down_perm)
        out = put(out, up, z - d * sign + NZ)
        out = put(out, down, z + d * sign + NZ)
    h = b // 2
    up = lax.ppermute(up[:h], "z", up_perm)
    down = lax.ppermute(down[h:], "z", down_perm)
    out = put(out, jnp.concatenate([up, down], axis=0), z + 4)
    return out.reshape(NZ * b, -1)


def activate(gate, up):
    return (jax.nn.silu(gate) * up).astype(BF16)


def times_t(a, b):
    return lax.dot_general(
        a,
        b,
        (((1,), (1,)), ((), ())),
        precision=lax.Precision.HIGHEST,
        preferred_element_type=F32,
    )


def scatter_rows(part):
    n = part.shape[0]
    pieces = exchange(part.astype(BF16).reshape(8, n // 8, -1))
    return jnp.sum(pieces.astype(F32), axis=0)


def per_device(
    tokens,
    table,
    gate_weight,
    up_weight,
    down_weight,
    gate_left,
    gate_right,
    up_left,
    up_right,
    down_left,
    down_right,
):
    z = lax.axis_index("z")
    b, rank = gate_right.shape[1], gate_right.shape[0]
    ff = gate_weight.shape[1]

    width = pack(
        jnp.concatenate([gate_left, up_left, down_right.T], axis=0), table.shape[1]
    )
    table_other = swap(table, "core")
    gates = gate_weight, swap(after(gate_weight, table_other), "core")
    ups = up_weight, swap(after(up_weight, table_other), "core")
    embedded, width, half, copies = embed(tokens, table, table_other, width)
    gate_l, up_l, down_r = unpack(width, 3, rank)

    def project(matrix):
        return jnp.dot(embedded, matrix, preferred_element_type=F32)

    columns = [
        project(gates[0]),
        project(ups[0]),
        project(gates[1]),
        project(ups[1]),
        project(jnp.concatenate([gate_l, up_l], axis=1)),
    ]

    pad = -b % 16
    gate_r, up_r, down_l, _ = lax.optimization_barrier(
        (gate_right, up_right, down_left, half)
    )
    units = jnp.stack(
        [jnp.pad(u, ((0, pad), (0, 0))) for u in (gate_r.T, up_r.T, down_l)]
    )
    units = gather_units(units, copies)
    units = units, swap(units[:, : 2 * (b + pad)], "core")

    def unit_rows(c, i):
        rows, lane = ((0, b + pad), i * rank) if i < 2 else ((2 * b + 2 * pad,) * 2, 0)
        halves = [
            units[c][:, r : r + b, k : k + rank]
            for r, k in ((rows[0], lane), (rows[1], lane + (rank if i == 2 else 0)))
        ]
        return jnp.stack(halves, axis=1).astype(F32).reshape(-1, rank)

    gate_rs = [unit_rows(c, 0) for c in range(2)]
    up_rs = [unit_rows(c, 1) for c in range(2)]
    gate_r, up_r, down_l = (
        u.astype(BF16) for u in (gate_rs[0], up_rs[0], unit_rows(0, 2))
    )
    merged_gate = merge_tile(gate_weight, gate_l, gate_r.T)
    merged_up = merge_tile(up_weight, up_l, up_r.T)
    merged_down = merge_tile(down_weight, down_l, down_r.T)
    downs = merged_down, swap(merged_down, "core")

    n = embedded.shape[0]
    streams = []
    for k in range(2):
        rows = slice(k * n // 2, (k + 1) * n // 2)
        sign = 1 - 2 * k
        mine = ring_scatter([c[rows] for c in columns], z, sign)
        total = mine + swap(mine.astype(BF16), "yh")
        gate, up, gate_o, up_o = (total[:, i * ff : (i + 1) * ff] for i in range(4))
        gate_t, up_t = 2.0 * total[:, 4 * ff : -rank], 2.0 * total[:, -rank:]
        hidden = jnp.concatenate(
            [
                activate(
                    gate + times_t(gate_t, gate_rs[0]), up + times_t(up_t, up_rs[0])
                ),
                activate(
                    gate_o + times_t(gate_t, gate_rs[1]), up_o + times_t(up_t, up_rs[1])
                ),
            ],
            axis=1,
        )
        streams.append(ring_gather(hidden, z, sign))
    hidden = jnp.concatenate(streams, axis=0)
    down = jnp.concatenate(downs, axis=0)
    result = jnp.dot(hidden, down, preferred_element_type=F32)
    return (scatter_rows(result), merged_gate, merged_up, merged_down)


def solution(mesh):
    fine = Mesh(mesh.devices.reshape(2, NX, 2, NZ, 2), ROW + COL)
    in_specs = (
        P(),
        P(ROW, COL),
        P(COL, ROW),
        P(COL, ROW),
        P(ROW, COL),
        P(COL + ROW, None),
        P(None, ROW + COL),
        P(COL + ROW, None),
        P(None, ROW + COL),
        P(ROW + COL, None),
        P(None, COL + ROW),
    )
    out_specs = (P(ROW, COL), P(COL, ROW), P(COL, ROW), P(ROW, COL))
    return jax.shard_map(
        per_device, mesh=fine, in_specs=in_specs, out_specs=out_specs, check_vma=False
    )
```

```python
import jax
import jax.numpy as jnp
from jax import lax
from jax.sharding import Mesh, PartitionSpec as P

BF16 = jnp.bfloat16
F32 = jnp.float32

NX, NZ = 4, 8
ROW = ("yl", "x", "core")
COL = ("z", "yh")


def shift(n, d):
    return [(i, (i + d) % n) for i in range(n)]


def flip(n, mask):
    return [(i, i ^ mask) for i in range(n)]


def swap(value, axis):
    return lax.ppermute(value, axis, flip(2, 1))


def after(value, *others):
    return lax.optimization_barrier((value, *others))[0]


def put(out, value, index):
    return lax.dynamic_update_index_in_dim(out, value, index % out.shape[0], 0)


def merge_tile(weight, left, right):
    delta = jnp.dot(left, right, preferred_element_type=F32)
    return (weight.astype(F32) + 2.0 * delta).astype(BF16)


def lookup(ids, table, base):
    local = ids - base
    hot = (local[:, None] == lax.broadcasted_iota(jnp.int32, (1, table.shape[0]), 1)).astype(BF16)
    return jnp.dot(hot, table, preferred_element_type=F32).astype(BF16)


def exchange(value):
    return lax.all_to_all(value, ("yl", "x"), 0, 0)


def pack(piece, width):
    groups = [piece[16 * k : 16 * (k + 1)] for k in range(piece.shape[0] // 16)]
    flat = jnp.concatenate(groups, axis=1)
    return jnp.pad(flat, ((0, 0), (0, width - flat.shape[1])))


def unpack(packed, count, rank):
    per = 3
    return [
        jnp.concatenate(
            [
                packed[:, :, rank * (per * i + k) : rank * (per * i + k + 1)]
                for k in range(per)
            ],
            axis=1,
        ).reshape(-1, rank)
        for i in range(count)
    ]


def gather_units(pieces, late):
    low = lax.axis_index("yh") == 0
    other = swap(pieces, "yh")
    pair = [jnp.where(low, pieces, other), jnp.where(low, other, pieces)]
    held = jnp.concatenate(
        [jnp.concatenate([p[0], p[1]], axis=1) for p in pair]
        + [jnp.concatenate([pair[0][2], pair[1][2]], axis=1)],
        axis=0,
    )
    shape = held.shape
    for mask in (4, 2, 1):
        if mask == 2:
            held = after(held, late)
        other = lax.ppermute(held, "z", flip(NZ, mask))
        low = lax.axis_index("z") & mask == 0
        held = jnp.stack([jnp.where(low, held, other), jnp.where(low, other, held)])
    return held.transpose(2, 1, 0, 3, 4).reshape((NZ,) + shape)


def embed(tokens, table, table_other, extra):
    core = lax.axis_index("core")
    vocab, wide = table.shape
    base = lax.axis_index(ROW) * vocab
    other_base = base + (1 - 2 * core) * vocab
    m = tokens.shape[0] // 16

    ids = tokens.reshape(8, 2, m)
    ids = lax.dynamic_index_in_dim(ids, core, axis=1, keepdims=False).reshape(-1)
    half = lookup(ids, table, base) + lookup(ids, table_other, other_base)
    pieces = exchange(half.reshape(8, m, wide))
    mine = pieces[0]
    for j in range(1, 8):
        mine = mine + pieces[j]
    mine = jnp.concatenate([mine, extra], axis=0)
    copies = lax.optimization_barrier(jnp.broadcast_to(mine[None], (8,) + mine.shape))
    every = exchange(copies)
    extras = every[:, m:]
    extras_other = swap(extras, "core")
    first = core == 0
    extras = jnp.stack(
        [
            jnp.where(first, extras, extras_other),
            jnp.where(first, extras_other, extras),
        ],
        axis=1,
    )
    rows = lax.optimization_barrier(every[:, :m].reshape(8 * m, wide))
    return rows, extras.reshape((16,) + extra.shape), half, copies


def ring_scatter(columns, z, sign):
    columns = [c.reshape(NZ, c.shape[0] // NZ, -1) for c in columns]
    up_perm, down_perm = shift(NZ, sign), shift(NZ, -sign)

    def add(index, held):
        index = (index + NZ) % NZ
        blocks = [
            lax.dynamic_index_in_dim(c, index, 0, keepdims=False) for c in columns
        ]
        whole = jnp.concatenate(blocks, axis=1)
        return whole if held is None else whole + held

    up = lax.ppermute(add(z + 4, None).astype(BF16), "z", up_perm)
    down = None
    for d in (3, 2, 1):
        up_next = add(z + d * sign, up).astype(BF16)
        down_next = add(z - d * sign, down).astype(BF16)
        up = lax.ppermute(up_next, "z", up_perm)
        down = lax.ppermute(down_next, "z", down_perm)
    return add(z, up) + down


def ring_gather(piece, z, sign):
    b = piece.shape[0]
    up_perm, down_perm = shift(NZ, sign), shift(NZ, -sign)
    out = put(jnp.zeros((NZ,) + piece.shape, piece.dtype), piece, z)
    up = down = piece
    for d in (1, 2, 3):
        up = lax.ppermute(up, "z", up_perm)
        down = lax.ppermute(down, "z", down_perm)
        out = put(out, up, z - d * sign + NZ)
        out = put(out, down, z + d * sign + NZ)
    h = b // 2
    up = lax.ppermute(up[:h], "z", up_perm)
    down = lax.ppermute(down[h:], "z", down_perm)
    out = put(out, jnp.concatenate([up, down], axis=0), z + 4)
    return out.reshape(NZ * b, -1)


def activate(gate, up):
    return (jax.nn.silu(gate) * up).astype(BF16)


def times_t(a, b):
    return lax.dot_general(
        a,
        b,
        (((1,), (1,)), ((), ())),
        precision=lax.Precision.HIGHEST,
        preferred_element_type=F32,
    )


def scatter_rows(part):
    n = part.shape[0]
    pieces = exchange(part.astype(BF16).reshape(8, n // 8, -1))
    return jnp.sum(pieces.astype(F32), axis=0)


def per_device(
    tokens,
    table,
    gate_weight,
    up_weight,
    down_weight,
    gate_left,
    gate_right,
    up_left,
    up_right,
    down_left,
    down_right,
):
    z = lax.axis_index("z")
    b, rank = gate_right.shape[1], gate_right.shape[0]
    ff = gate_weight.shape[1]

    width = pack(
        jnp.concatenate([gate_left, up_left, down_right.T], axis=0), table.shape[1]
    )
    table_other = swap(table, "core")
    gates = gate_weight, swap(after(gate_weight, table_other), "core")
    ups = up_weight, swap(after(up_weight, table_other), "core")
    embedded, width, half, copies = embed(tokens, table, table_other, width)
    gate_l, up_l, down_r = unpack(width, 3, rank)

    def project(matrix):
        return jnp.dot(embedded, matrix, preferred_element_type=F32)

    columns = [
        project(gates[0]),
        project(ups[0]),
        project(gates[1]),
        project(ups[1]),
        project(jnp.concatenate([gate_l, up_l], axis=1)),
    ]

    columns = lax.optimization_barrier(columns)
    pad = -b % 16
    gate_r, up_r, down_l, _ = lax.optimization_barrier(
        (gate_right, up_right, down_left, half)
    )
    units = jnp.stack(
        [jnp.pad(u, ((0, pad), (0, 0))) for u in (gate_r.T, up_r.T, down_l)]
    )
    units = gather_units(units, copies)
    units = units, swap(units[:, : 2 * (b + pad)], "core")

    def unit_rows(c, i):
        rows, lane = ((0, b + pad), i * rank) if i < 2 else ((2 * b + 2 * pad,) * 2, 0)
        halves = [
            units[c][:, r : r + b, k : k + rank]
            for r, k in ((rows[0], lane), (rows[1], lane + (rank if i == 2 else 0)))
        ]
        return jnp.stack(halves, axis=1).astype(F32).reshape(-1, rank)

    gate_rs = [unit_rows(c, 0) for c in range(2)]
    up_rs = [unit_rows(c, 1) for c in range(2)]
    gate_r, up_r, down_l = (
        u.astype(BF16) for u in (gate_rs[0], up_rs[0], unit_rows(0, 2))
    )
    merged_gate = merge_tile(gate_weight, gate_l, gate_r.T)
    merged_up = merge_tile(up_weight, up_l, up_r.T)
    merged_down = merge_tile(down_weight, down_l, down_r.T)
    downs = merged_down, swap(merged_down, "core")

    n = embedded.shape[0]
    streams = []
    for k in range(2):
        rows = slice(k * n // 2, (k + 1) * n // 2)
        sign = 1 - 2 * k
        mine = ring_scatter([c[rows] for c in columns], z, sign)
        total = mine + swap(mine.astype(BF16), "yh")
        gate, up, gate_o, up_o = (total[:, i * ff : (i + 1) * ff] for i in range(4))
        gate_t, up_t = 2.0 * total[:, 4 * ff : -rank], 2.0 * total[:, -rank:]
        hidden = jnp.concatenate(
            [
                activate(
                    gate + times_t(gate_t, gate_rs[0]), up + times_t(up_t, up_rs[0])
                ),
                activate(
                    gate_o + times_t(gate_t, gate_rs[1]), up_o + times_t(up_t, up_rs[1])
                ),
            ],
            axis=1,
        )
        streams.append(ring_gather(hidden, z, sign))
    hidden = jnp.concatenate(streams, axis=0)
    down = jnp.concatenate(downs, axis=0)
    result = jnp.dot(hidden, down, preferred_element_type=F32)
    return (scatter_rows(result), merged_gate, merged_up, merged_down)


def solution(mesh):
    fine = Mesh(mesh.devices.reshape(2, NX, 2, NZ, 2), ROW + COL)
    in_specs = (
        P(),
        P(ROW, COL),
        P(COL, ROW),
        P(COL, ROW),
        P(ROW, COL),
        P(COL + ROW, None),
        P(None, ROW + COL),
        P(COL + ROW, None),
        P(None, ROW + COL),
        P(ROW + COL, None),
        P(None, COL + ROW),
    )
    out_specs = (P(ROW, COL), P(COL, ROW), P(COL, ROW), P(ROW, COL))
    return jax.shard_map(
        per_device, mesh=fine, in_specs=in_specs, out_specs=out_specs, check_vma=False
    )
```
